256 devices in a mesh: store: 8 (over z), grp: 4 (over y), tile: 8 (over x, core).
Axes of the slice: x: 4, y: 4, z: 8, core: 2. Of those that a mesh axis runs over, the one named last changes fastest.
Arguments:
- embeddings: bfloat16 [65536, 1024], P(('store', 'tile')), may hold values from -70 to 70, as said below
- storage_owner: int32 [4, 16384, 1], P('grp', ('store', 'tile')), may hold values from 0 to 63; in each aligned block of 256 rows (0 to 255, 256 to 511, ..., all dimensions but the last counted through in order) at most 8 rows name the same one
- local_row: int32 [4, 16384], P('grp', ('store', 'tile')), may hold values from 0 to 1023
- member_rank: int32 [4, 16384], P('grp', ('store', 'tile')), may hold values from 0 to 16383, each once within a row
- cluster_size: int32 [4], P('grp'), may hold values from 1 to 16384, 40960 in all
Outputs:
- best_similarity: float32 [4, 16384], P('grp', ('store', 'tile'))
The draws below stay inside these ranges and needn't reach their ends.
Inputs may be any that keep to these rules, and one draw needn't show every extreme that they name: `storage_owner`: among the slots of one device (256 aligned slots of a cluster), no storage device is named more than 8 times, and some storage device exactly 8 times. `member_rank`: each cluster's ranks name every number below 16384 once. `cluster_size`: the largest cluster size is exactly 16384. `embeddings`: rows are nonzero.
All inputs are finite; a program needn't handle non-finite values. No bound on the sum of `cluster_size` on one device may be relied on, other than what follows from the above.
Results may differ from the reference program's by a relative error of at most 0.0007.
Values may be sent and summed in bfloat16 or wider, within the bound.
No kernel may reach another device: no remote copies, remote signals or barrier semaphores. Data moves between devices by JAX's collectives and lax.ppermute only.
A program may use at most 64 MiB of HBM per device.

```python
import math
import jax
import jax.numpy as jnp
import numpy as np
from jax import lax

D = 1024
MEM_DEV = 256
ROWS_DEV = 1024
CLUSTERS = 4
MEMBERS = 16384
IDS = 65536
CAP = 8
N_STORE = 8
N_TILE = 8


def draw_embeddings(key, part):
    key = jax.random.fold_in(key, 7)
    first, second, third = jax.random.split(key, 3)
    partner = jax.random.permutation(second, IDS)
    mixing = jax.random.uniform(third, (IDS, 1), jnp.float32, 0.0, 3.0)
    base = jax.random.truncated_normal(first, -6.0, 6.0, (IDS, D), jnp.float32)
    mixed = base + mixing * jnp.take(base, partner, axis=0)
    return mixed.astype(jnp.bfloat16)


def set_ends(array, key, least, largest):
    spot = [jax.random.randint(jax.random.fold_in(key, axis), (), 0, length) for axis, length in enumerate(array.shape)]
    main_axis = array.shape.index(max(array.shape))
    neighbour = spot[:main_axis] + [(spot[main_axis] + 1) % array.shape[main_axis]] + spot[main_axis + 1:]
    return array.at[tuple(spot)].set(least).at[tuple(neighbour)].set(largest)


def profile(count, total, bound, slope):
    portions = [(1 << 20) // math.isqrt(rank ** slope) + 1 for rank in range(2, count + 1)]
    rest, holding = total - bound - (count - 1), [1] * (count - 1)
    while rest > 0:
        candidates = [i for i in range(count - 1) if holding[i] < bound]
        mass, remaining = sum([portions[i] for i in candidates]), rest
        for i in candidates:
            addition = min(bound - holding[i], max(1, remaining * portions[i] // mass), rest)
            holding[i] = holding[i] + addition
            rest = rest - addition
    return np.array([bound] + holding)


def uneven_parts(own_key, amount, total, limit, slope):
    if amount == 2:
        one = jax.random.randint(own_key, (), max(1, total - limit), min(limit, total - 1) + 1)
        return jnp.stack([one, total - one])
    tallies = jnp.asarray(profile(amount, total, limit, slope), jnp.int32)
    twos = (amount - 1) // 2
    giver, taker = tallies[1:1 + 2 * twos:2], tallies[2:2 + 2 * twos:2]
    slack = jnp.minimum(giver - 1, limit - taker)
    moved = jax.random.randint(jax.random.fold_in(own_key, 1), (twos,), 0, 1 << 20) % (slack + 1)
    tallies = tallies.at[1:1 + 2 * twos:2].set(giver - moved).at[2:2 + 2 * twos:2].set(taker + moved)
    return tallies[jax.random.permutation(jax.random.fold_in(own_key, 2), amount)]


def assign_block(own_key, own, number, rows, number_of, top, bound, skew):
    ranking = jax.random.permutation(own_key, number_of)
    packed, usual = load_shares(number_of, rows * top, bound, skew, True), load_shares(number_of, rows * top, bound, skew, False)
    places = jnp.arange(number_of)

    def named(lengths, turn):
        used = int((lengths > 0).sum())
        fixed = max(1, used // 4)
        shifted = fixed + (places - fixed + turn * (used - fixed)) % max(1, number_of - fixed)
        return jnp.zeros((number_of,), jnp.int32).at[ranking[jnp.where(places < fixed, places, shifted)]].set(jnp.asarray(lengths, jnp.int32))

    lengths = jnp.where(number % 4 == 0, named(packed, number // 4), named(usual, number - number // 4 - 1))
    mixed = jax.random.permutation(jax.random.fold_in(own, 3), number_of)
    source_of, receiver = mixed[0:number_of // 2 * 2:2], mixed[1:number_of // 2 * 2:2]
    room = jnp.minimum(lengths[source_of] - 1, bound - lengths[receiver]) // 2
    room = jnp.where((source_of == ranking[0]) | (receiver == ranking[0]) | (lengths[receiver] == 0), 0, jnp.maximum(room, 0))
    shifted = jax.random.randint(jax.random.fold_in(own, 4), (number_of // 2,), 0, 1 << 20) % (room + 1)
    lengths = lengths.at[source_of].add(-shifted).at[receiver].add(shifted)
    items = jnp.searchsorted(jnp.cumsum(lengths), jnp.arange(rows * top), side="right").astype(jnp.int32)
    listing = items.reshape(top, rows).T
    listing = listing[jax.random.permutation(jax.random.fold_in(own, 1), rows)]
    turn = jax.random.randint(jax.random.fold_in(own, 2), (rows, 1), 0, top)
    return jnp.take_along_axis(listing, (jnp.arange(top)[None, :] + turn) % top, axis=1)


def load_shares(count, total, reach, slope, full):
    weights = [(1 << 20) // math.isqrt(standing ** slope) + 1 for standing in range(1, count + 1)]
    largest = reach if full else min(reach, max(-(-total // count), total * weights[0] // sum(weights)))
    least = 1 if total - largest >= count - 1 else 0
    given, spare = [largest] + [least] * (count - 1), total - largest - least * (count - 1)
    while spare > 0:
        movable = [i for i in range(1, count) if given[i] < largest] or [i for i in range(1, count) if given[i] < reach]
        whole, remaining = sum([weights[i] for i in movable]), spare
        for i in movable:
            extra = min(reach - given[i], max(1, remaining * weights[i] // whole), spare)
            given[i] = given[i] + extra
            spare = spare - extra
    return np.array(given)


def setup_inputs(seed: int = 0) -> dict:
    arg_keys = jax.random.split(jax.random.key(seed), 6)
    embeddings = draw_embeddings(jax.random.fold_in(arg_keys[5], 71), 0)
    storage_owner_keys = jax.random.split(jax.random.fold_in(arg_keys[1], 1), CLUSTERS * MEMBERS // MEM_DEV)
    storage_owner_turns = jax.random.permutation(jax.random.fold_in(arg_keys[1], 3), CLUSTERS * MEMBERS // MEM_DEV)
    storage_owner = jax.vmap(lambda own, number: assign_block(jax.random.fold_in(arg_keys[1], 2), own, number, MEM_DEV, N_STORE * N_TILE, 1, CAP, 2))(storage_owner_keys, storage_owner_turns).reshape((CLUSTERS, MEMBERS, 1))
    local_row = set_ends(jax.random.randint(arg_keys[2], (CLUSTERS, MEMBERS), 0, ROWS_DEV), jax.random.fold_in(arg_keys[2], 1), 0, ROWS_DEV - 1).astype(jnp.int32)
    member_rank = jax.vmap(lambda own: jax.random.permutation(own, MEMBERS))(jax.random.split(arg_keys[3], CLUSTERS)).reshape((CLUSTERS, MEMBERS)).astype(jnp.int32)
    cluster_size = uneven_parts(arg_keys[4], CLUSTERS, CLUSTERS * MEMBERS * 5 // 8, MEMBERS, 2).astype(jnp.int32)
    return dict(embeddings=embeddings, storage_owner=storage_owner, local_row=local_row, member_rank=member_rank, cluster_size=cluster_size)


def unit_rows(table):
    wide = table.astype(jnp.float32)
    total = lax.optimization_barrier(jnp.sum(wide * wide, axis=-1, keepdims=True)) + 1e-06
    return (wide * lax.rsqrt(total)).astype(jnp.bfloat16)

def reference(embeddings, storage_owner, local_row, member_rank, cluster_size):
    results = []
    for cluster in range(CLUSTERS):
        member_ids = storage_owner[cluster, :, 0] * ROWS_DEV + local_row[cluster]
        normed = unit_rows(jnp.take(embeddings, member_ids, axis=0))
        ranks = member_rank[cluster]
        live = jnp.arange(MEMBERS, dtype=jnp.int32) < cluster_size[cluster]

        def one_block(index):
            first = (index * MEM_DEV).astype(jnp.int32)
            block_rows = lax.dynamic_slice_in_dim(normed, first, MEM_DEV, 0)
            block_rank = lax.dynamic_slice_in_dim(ranks, first, MEM_DEV, 0)
            scores = jnp.dot(block_rows, normed.T, preferred_element_type=jnp.float32)
            allowed = (ranks[None, :] < block_rank[:, None]) & live[None, :]
            return lax.optimization_barrier(jnp.max(jnp.where(allowed, scores, jnp.float32(-1.0)), axis=1))
        highest = lax.map(one_block, jnp.arange(MEMBERS // MEM_DEV, dtype=jnp.int32)).reshape(-1)
        results.append(jnp.where(live, highest, jnp.float32(0.0)))
    return jnp.stack(results)
```

```python
import functools

import jax
import jax.numpy as jnp
from jax import lax
from jax.experimental import pallas as pl
from jax.experimental.pallas import tpu as pltpu
from jax.sharding import PartitionSpec as P

EXTRA = 16


def unit_rows(table):
    wide = table.astype(jnp.float32)
    total = jnp.sum(wide * wide, axis=-1, keepdims=True) + 1e-06
    return (wide * lax.rsqrt(total)).astype(jnp.bfloat16)


def to_column(row):
    return jnp.broadcast_to(row, (128, row.shape[1])).T


def compact_kernel(back_ref, target_ref, rank_ref, out_ref):
    slots = target_ref.shape[1]
    held = back_ref.shape[0]
    width = back_ref.shape[1]
    column = to_column(target_ref[...].astype(jnp.float32))[:, :1]
    place = lax.broadcasted_iota(jnp.int32, (slots, held), 1).astype(jnp.float32)
    pick = (column == place).astype(jnp.bfloat16)
    out_ref[0:slots, :] = jnp.dot(
        pick, back_ref[...], preferred_element_type=jnp.float32
    ).astype(jnp.bfloat16)
    rank = rank_ref[...]
    high = (rank >> 7).astype(jnp.float32)
    low = (rank & 127).astype(jnp.float32)
    line = jnp.concatenate(
        [high, low, jnp.zeros((1, width - 2 * slots), jnp.float32)], axis=1
    )
    out_ref[slots : slots + EXTRA, :] = jnp.broadcast_to(line, (EXTRA, width)).astype(
        jnp.bfloat16
    )


def compact(back, target, rank):
    slots = target.shape[0]
    return pl.pallas_call(
        compact_kernel,
        out_shape=jax.ShapeDtypeStruct((slots + EXTRA, back.shape[1]), jnp.bfloat16),
        compiler_params=pltpu.CompilerParams(vmem_limit_bytes=24 * 1024 * 1024),
        cost_estimate=pl.CostEstimate(
            flops=2 * slots * back.shape[0] * back.shape[1],
            bytes_accessed=4 * back.size,
            transcendentals=0,
        ),
    )(back, target[None], rank[None])


def rank_row(ref, slots):
    line = ref[slots : slots + EXTRA, :][0:1].astype(jnp.float32)
    return line[:, 0:slots] * 128.0 + line[:, slots : 2 * slots]


def score_kernel(n_rows, n_cols, with_col, slots, *refs):
    row_refs = refs[:n_rows]
    col_refs = refs[n_rows : n_rows + n_cols]
    row_out = refs[n_rows + n_cols]
    col_out = refs[n_rows + n_cols + 1] if any(with_col) else None
    col_rank = [rank_row(ref, slots) for ref in col_refs]
    col_best = [jnp.full((8, slots), -1.0, jnp.float32) for _ in col_refs]
    for j, row_ref in enumerate(row_refs):
        own = to_column(rank_row(row_ref, slots))
        own = jnp.concatenate([own, own], axis=1)
        best = jnp.full((slots, 128), -1.0, jnp.float32)
        for i, col_ref in enumerate(col_refs):
            score = lax.dot_general(
                row_ref[0:slots, :],
                col_ref[0:slots, :],
                (((1,), (1,)), ((), ())),
                preferred_element_type=jnp.float32,
            )
            masked = jnp.where(col_rank[i] < own, score, -1.0)
            best = jnp.maximum(best, jnp.maximum(masked[:, :128], masked[:, 128:]))
            if with_col[i]:
                masked = jnp.where(own < col_rank[i], score, -1.0)
                folded = jnp.max(masked.reshape(slots // 8, 8, slots), axis=0)
                col_best[i] = jnp.maximum(col_best[i], folded)
        row_out[j : j + 1, :] = jnp.max(best.T, axis=0, keepdims=True)
    place = 0
    for i in range(n_cols):
        if with_col[i]:
            col_out[place : place + 1, :] = jnp.max(col_best[i], axis=0, keepdims=True)
            place += 1


def score(rows, cols, with_col):
    slots = rows[0].shape[0] - EXTRA
    width = rows[0].shape[1]
    out = [jax.ShapeDtypeStruct((len(rows), slots), jnp.float32)]
    if any(with_col):
        out.append(jax.ShapeDtypeStruct((sum(with_col), slots), jnp.float32))
    return pl.pallas_call(
        functools.partial(score_kernel, len(rows), len(cols), tuple(with_col), slots),
        out_shape=out,
        compiler_params=pltpu.CompilerParams(vmem_limit_bytes=40 * 1024 * 1024),
        cost_estimate=pl.CostEstimate(
            flops=2 * len(rows) * len(cols) * slots * slots * width,
            bytes_accessed=2 * (len(rows) + len(cols)) * slots * width,
            transcendentals=0,
        ),
    )(*rows, *cols)


def on_device(embeddings, storage_owner, local_row, member_rank, cluster_size):
    n_store = lax.axis_size("store")
    n_tile = lax.axis_size("tile")
    peers = n_store * n_tile
    slots = local_row.shape[1]
    width = embeddings.shape[1]
    cap = 2 * slots // peers
    owner = storage_owner[0, :, 0]
    local = local_row[0]
    s_index = lax.axis_index("store")
    t_index = lax.axis_index("tile")
    own_slot = (s_index * n_tile + t_index) * slots + jnp.arange(slots, dtype=jnp.int32)
    live = own_slot < cluster_size[0]
    rank = jnp.where(live, member_rank[0], jnp.int32(n_store * n_tile * slots))

    index = jnp.arange(slots, dtype=jnp.int32)
    earlier = (owner[:, None] == owner[None, :]) & (index[:, None] < index[None, :])
    target = owner * cap + jnp.sum(earlier.astype(jnp.int32), axis=0)
    places = jnp.arange(peers * cap, dtype=jnp.int32)
    requests = jnp.sum(
        jnp.where(target[None, :] == places[:, None], local[None, :], 0), axis=1
    ).reshape(peers, cap)

    both = ("store", "tile")
    asked = lax.all_to_all(requests, both, split_axis=0, concat_axis=0, tiled=True)
    table = unit_rows(embeddings)
    found = jnp.take(table, asked.reshape(-1), axis=0).reshape(peers, cap, width)
    back = lax.all_to_all(found, both, split_axis=0, concat_axis=0, tiled=True)
    block = compact(back.reshape(peers * cap, width), target, rank)

    def z_move(array, by):
        return lax.ppermute(
            array, "store", [(i, (i + by) % n_store) for i in range(n_store)]
        )

    def x_move(array, by):
        return lax.ppermute(
            array, "tile", [(i, (i + 2 * by) % n_tile) for i in range(n_tile)]
        )

    def zx_move(array, z_by, x_by):
        pairs = []
        for z in range(n_store):
            for i in range(n_tile):
                to = (z + z_by) % n_store * n_tile + (i + 2 * x_by) % n_tile
                pairs.append((z * n_tile + i, to))
        return lax.ppermute(array, both, pairs)

    def core_move(array):
        return lax.ppermute(array, "tile", [(i, i ^ 1) for i in range(n_tile)])

    next_plane = z_move(block, -1)
    back_one = z_move(block, 1)
    back_two = z_move(back_one, 1)
    back_three = z_move(back_two, 1)
    half = slots // 2
    from_left = x_move(next_plane, 1)
    from_right = x_move(next_plane, -1)
    across = jnp.concatenate(
        [x_move(from_left[:half], 1), x_move(from_right[half:], -1)], axis=0
    )
    rows = [next_plane, from_left, from_right, across]
    rows = rows + [core_move(r) for r in rows]

    row_best, col_best = score(
        rows, [next_plane, block, back_one, back_two], [False, True, True, True]
    )
    (row_last,) = score(rows, [back_three], [False])
    row_best = jnp.maximum(row_best, row_last)

    mine = jnp.maximum(row_best[0:4], core_move(row_best[4:8]))
    parts = [
        col_best[0],
        z_move(col_best[1], -1),
        z_move(col_best[2], -2),
        zx_move(mine[0], 1, 0),
        zx_move(mine[1], 1, -1),
        zx_move(mine[2], 1, 1),
        zx_move(mine[3], 1, 2),
    ]
    highest = functools.reduce(jnp.maximum, parts)
    return jnp.where(live, highest, jnp.float32(0.0))[None]


def solution(mesh):
    placed = (
        P(("store", "tile"), None),
        P("grp", ("store", "tile"), None),
        P("grp", ("store", "tile")),
        P("grp", ("store", "tile")),
        P("grp"),
    )
    return jax.shard_map(
        on_device,
        mesh=mesh,
        in_specs=placed,
        out_specs=P("grp", ("store", "tile")),
        check_vma=False,
    )
```

```python
import functools

import jax
import jax.numpy as jnp
from jax import lax
from jax.experimental import pallas as pl
from jax.experimental.pallas import tpu as pltpu
from jax.sharding import PartitionSpec as P

EXTRA = 16


def unit_rows(table):
    wide = table.astype(jnp.float32)
    total = jnp.sum(wide * wide, axis=-1, keepdims=True) + 1e-06
    return (wide * lax.rsqrt(total)).astype(jnp.bfloat16)


def to_column(row):
    return jnp.broadcast_to(row, (128, row.shape[1])).T


def request_kernel(owner_ref, local_ref, ask_ref, target_ref, *, cap):
    slots = owner_ref.shape[1]
    peers = ask_ref.shape[0]
    lanes = ask_ref.shape[2]
    owner = owner_ref[...].astype(jnp.float32)
    local = local_ref[...]
    column = to_column(owner)
    same = jnp.concatenate([column] * (slots // 128), axis=1) == owner
    first = lax.broadcasted_iota(jnp.int32, (slots, slots), 0)
    second = lax.broadcasted_iota(jnp.int32, (slots, slots), 1)
    before = jnp.where(same & (first < second), 1.0, 0.0)
    position = jnp.sum(before, axis=0, keepdims=True)
    target_ref[...] = (owner * cap + position).astype(jnp.int32)
    peer = lax.broadcasted_iota(jnp.int32, (peers, slots), 0).astype(jnp.float32)
    of_peer = jnp.where(peer == owner, 1.0, 0.0).astype(jnp.bfloat16)
    lane = lax.broadcasted_iota(jnp.int32, (slots, lanes), 1).astype(jnp.float32)
    here = to_column(position) == lane
    high = to_column((local >> 5).astype(jnp.float32))
    low = to_column((local & 31).astype(jnp.float32))
    parts = jnp.concatenate(
        [jnp.where(here, high, 0.0), jnp.where(here, low, 0.0)], axis=1
    ).astype(jnp.bfloat16)
    found = jnp.dot(of_peer, parts, preferred_element_type=jnp.float32)
    ask_ref[:, 0, :] = (found[:, :lanes] * 32.0 + found[:, lanes:]).astype(jnp.int32)


def request(owner, local, peers, cap):
    slots = owner.shape[1]
    return pl.pallas_call(
        functools.partial(request_kernel, cap=cap),
        out_shape=[
            jax.ShapeDtypeStruct((peers, 1, 128), jnp.int32),
            jax.ShapeDtypeStruct((1, slots), jnp.int32),
        ],
    )(owner, local)


def lookup_kernel(asked_ref, table_ref, out_ref, *, cap):
    peers = asked_ref.shape[0]
    lanes = asked_ref.shape[2]
    held = table_ref.shape[0]
    count = out_ref.shape[0]
    asked = asked_ref[:, 0, :]
    parts = jnp.concatenate(
        [(asked >> 5).astype(jnp.float32), (asked & 31).astype(jnp.float32)], axis=1
    ).astype(jnp.bfloat16)
    place = lax.broadcasted_iota(jnp.int32, (count, peers), 0)
    peer = lax.broadcasted_iota(jnp.int32, (count, peers), 1)
    spread = jnp.where(place // cap == peer, 1.0, 0.0).astype(jnp.bfloat16)
    both = jnp.dot(spread, parts, preferred_element_type=jnp.float32)
    both = both[:, :lanes] * 32.0 + both[:, lanes:]
    place = lax.broadcasted_iota(jnp.int32, (count, lanes), 0)
    lane = lax.broadcasted_iota(jnp.int32, (count, lanes), 1)
    wanted = jnp.sum(jnp.where(place % cap == lane, both, 0.0), axis=1, keepdims=True)
    column = lax.broadcasted_iota(jnp.int32, (count, held), 1).astype(jnp.float32)
    pick = jnp.where(wanted == column, 1.0, 0.0).astype(jnp.bfloat16)
    out_ref[...] = jnp.dot(
        pick, table_ref[...], preferred_element_type=jnp.float32
    ).astype(jnp.bfloat16)


def lookup(asked, table, cap):
    count = asked.shape[0] * cap
    return pl.pallas_call(
        functools.partial(lookup_kernel, cap=cap),
        out_shape=jax.ShapeDtypeStruct((count, table.shape[1]), jnp.bfloat16),
        compiler_params=pltpu.CompilerParams(vmem_limit_bytes=24 * 1024 * 1024),
        cost_estimate=pl.CostEstimate(
            flops=2 * count * table.size, bytes_accessed=4 * table.size, transcendentals=0
        ),
    )(asked, table)


def compact_kernel(back_ref, target_ref, rank_ref, out_ref):
    slots = target_ref.shape[1]
    held = back_ref.shape[0]
    width = back_ref.shape[1]
    column = to_column(target_ref[...].astype(jnp.float32))[:, :1]
    place = lax.broadcasted_iota(jnp.int32, (slots, held), 1).astype(jnp.float32)
    pick = (column == place).astype(jnp.bfloat16)
    out_ref[0:slots, :] = jnp.dot(
        pick, back_ref[...], preferred_element_type=jnp.float32
    ).astype(jnp.bfloat16)
    rank = rank_ref[...]
    high = (rank >> 7).astype(jnp.float32)
    low = (rank & 127).astype(jnp.float32)
    line = jnp.concatenate(
        [high, low, jnp.zeros((1, width - 2 * slots), jnp.float32)], axis=1
    )
    out_ref[slots : slots + EXTRA, :] = jnp.broadcast_to(line, (EXTRA, width)).astype(
        jnp.bfloat16
    )


def compact(back, target, rank):
    slots = target.shape[1]
    return pl.pallas_call(
        compact_kernel,
        out_shape=jax.ShapeDtypeStruct((slots + EXTRA, back.shape[1]), jnp.bfloat16),
        compiler_params=pltpu.CompilerParams(vmem_limit_bytes=24 * 1024 * 1024),
        cost_estimate=pl.CostEstimate(
            flops=2 * slots * back.shape[0] * back.shape[1],
            bytes_accessed=4 * back.size,
            transcendentals=0,
        ),
    )(back, target, rank)


def rank_row(ref, slots):
    line = ref[slots : slots + EXTRA, :][0:1].astype(jnp.float32)
    return line[:, 0:slots] * 128.0 + line[:, slots : 2 * slots]


def scores_of(row_refs, col_refs, col_only, with_col, slots):
    col_rank = [rank_row(ref, slots) for ref in col_refs]
    col_best = [jnp.full((8, slots), -1.0, jnp.float32) for _ in col_refs]
    row_best = []
    for row_ref in row_refs:
        own = to_column(rank_row(row_ref, slots))
        own = jnp.concatenate([own] * (slots // 128), axis=1)
        best = jnp.full((slots, 128), -1.0, jnp.float32)
        for i, col_ref in enumerate(col_refs):
            score = lax.dot_general(
                row_ref[0:slots, :],
                col_ref[0:slots, :],
                (((1,), (1,)), ((), ())),
                preferred_element_type=jnp.float32,
            )
            if not col_only:
                masked = jnp.where(col_rank[i] < own, score, -1.0)
                for k in range(slots // 128):
                    best = jnp.maximum(best, masked[:, 128 * k : 128 * (k + 1)])
            if with_col[i]:
                masked = jnp.where(own < col_rank[i], score, -1.0)
                folded = jnp.max(masked.reshape(slots // 8, 8, slots), axis=0)
                col_best[i] = jnp.maximum(col_best[i], folded)
        row_best.append(None if col_only else jnp.max(best.T, axis=0, keepdims=True))
    kept = [
        jnp.max(best, axis=0, keepdims=True)
        for best, wanted in zip(col_best, with_col)
        if wanted
    ]
    return row_best, kept


def first_kernel(*refs, slots):
    row_out, col_out = refs[8:]
    rows, cols = scores_of(refs[:4], refs[4:8], False, (False, True, True, True), slots)
    for j in range(4):
        row_out[j : j + 1, :] = rows[j]
    for j in range(3):
        col_out[j : j + 1, :] = cols[j]


def second_kernel(*refs, slots):
    row_in, col_in, own_out, other_out, col_out = refs[8:]
    rows, cols = scores_of(refs[:4], refs[4:8], False, (False, True, True, True), slots)
    own_out[0:3, :] = row_in[0:3, :]
    own_out[3:4, :] = rows[0]
    other_out[0:1, :] = row_in[3:4, :]
    for j in range(3):
        other_out[j + 1 : j + 2, :] = rows[j + 1]
        col_out[j : j + 1, :] = jnp.maximum(col_in[j : j + 1, :], cols[j])


def last_kernel(*refs, slots):
    _, cols = scores_of(refs[:8], refs[8:9], True, (True,), slots)
    refs[9][...] = cols[0]


def score(kernel, blocks, extra, shapes, pairs):
    slots = blocks[0].shape[0] - EXTRA
    width = blocks[0].shape[1]
    return pl.pallas_call(
        functools.partial(kernel, slots=slots),
        out_shape=[jax.ShapeDtypeStruct((n, slots), jnp.float32) for n in shapes],
        compiler_params=pltpu.CompilerParams(vmem_limit_bytes=40 * 1024 * 1024),
        cost_estimate=pl.CostEstimate(
            flops=2 * pairs * slots * slots * width,
            bytes_accessed=2 * len(blocks) * slots * width,
            transcendentals=0,
        ),
    )(*blocks, *extra)


def on_device(embeddings, storage_owner, local_row, member_rank, cluster_size):
    n_store = lax.axis_size("store")
    n_tile = lax.axis_size("tile")
    peers = n_store * n_tile
    slots = local_row.shape[1]
    width = embeddings.shape[1]
    cap = 2 * slots // peers
    both = ("store", "tile")
    s_index = lax.axis_index("store")
    t_index = lax.axis_index("tile")

    requests, target = request(storage_owner[:, :, 0], local_row, peers, cap)
    asked = lax.all_to_all(requests, both, split_axis=0, concat_axis=0, tiled=True)
    own_slot = (s_index * n_tile + t_index) * slots + jnp.arange(slots, dtype=jnp.int32)
    live = (own_slot < cluster_size[0])[None]
    rank = jnp.where(live, member_rank, jnp.int32(peers * slots))
    table = unit_rows(embeddings)
    found = lookup(asked, table, cap).reshape(peers, cap, width)
    back = lax.all_to_all(found, both, split_axis=0, concat_axis=0, tiled=True)
    block = compact(back.reshape(peers * cap, width), target, rank)

    def z_move(array, by):
        return lax.ppermute(
            array, "store", [(i, (i + by) % n_store) for i in range(n_store)]
        )

    def t_move(array, flip):
        return lax.ppermute(array, "tile", [(i, i ^ flip) for i in range(n_tile)])

    def zt_move(array, z_by, flip):
        pairs = []
        for z in range(n_store):
            for i in range(n_tile):
                pairs.append((z * n_tile + i, (z + z_by) % n_store * n_tile + (i ^ flip)))
        return lax.ppermute(array, both, pairs)

    near = z_move(block, -1)
    back_one = z_move(block, 1)
    near, back_one = lax.optimization_barrier((near, back_one))
    back_two = z_move(back_one, 1)
    x_one = t_move(near, 2)
    x_three = t_move(near, 6)
    near_other = t_move(near, 1)
    back_two, x_one, x_three, near_other = lax.optimization_barrier(
        (back_two, x_one, x_three, near_other)
    )
    back_three = z_move(back_two, 1)
    half = slots // 2
    x_two = jnp.concatenate(
        [t_move(x_one[:half], 6), t_move(x_three[half:], 2)], axis=0
    )
    x_one_other = t_move(x_one, 1)
    x_three_other = t_move(x_three, 1)
    x_two_other = t_move(x_two, 1)

    cols = [near, block, back_one, back_two]
    early = [near, x_one, x_three, near_other]
    late = [x_two, x_one_other, x_three_other, x_two_other]
    row_best, col_best = score(first_kernel, early + cols, [], [4, 3], 16)
    mine, other, col_best = score(
        second_kernel, late + cols, [row_best, col_best], [4, 4, 3], 16
    )
    (col_last,) = score(last_kernel, early + late + [back_three], [], [1], 8)

    mine = jnp.maximum(mine, t_move(other, 1))
    passed = t_move(mine[1:3], 2)
    parts = [
        col_best[0:1],
        z_move(col_best[1:2], -1),
        z_move(col_best[2:3], -2),
        zt_move(jnp.maximum(mine[0:1], passed[0:1]), 1, 0),
        zt_move(jnp.maximum(mine[3:4], passed[1:2]), 1, 4),
        z_move(col_last, -3),
    ]
    highest = functools.reduce(jnp.maximum, parts)
    return jnp.where(live, highest, jnp.float32(0.0))


def solution(mesh):
    placed = (
        P(("store", "tile"), None),
        P("grp", ("store", "tile"), None),
        P("grp", ("store", "tile")),
        P("grp", ("store", "tile")),
        P("grp"),
    )
    return jax.shard_map(
        on_device,
        mesh=mesh,
        in_specs=placed,
        out_specs=P("grp", ("store", "tile")),
        check_vma=False,
    )
```

```python
import functools

import jax
import jax.numpy as jnp
from jax import lax
from jax.experimental import pallas as pl
from jax.experimental.pallas import tpu as pltpu
from jax.sharding import PartitionSpec as P

EXTRA = 16


def unit_rows(table):
    wide = table.astype(jnp.float32)
    total = jnp.sum(wide * wide, axis=-1, keepdims=True) + 1e-06
    return (wide * lax.rsqrt(total)).astype(jnp.bfloat16)


def to_column(row):
    return jnp.broadcast_to(row, (128, row.shape[1])).T


def request_kernel(owner_ref, local_ref, ask_ref, target_ref, *, cap):
    slots = owner_ref.shape[1]
    peers = ask_ref.shape[0]
    lanes = ask_ref.shape[2]
    owner = owner_ref[...].astype(jnp.float32)
    local = local_ref[...]
    column = to_column(owner)
    same = jnp.concatenate([column] * (slots // 128), axis=1) == owner
    first = lax.broadcasted_iota(jnp.int32, (slots, slots), 0)
    second = lax.broadcasted_iota(jnp.int32, (slots, slots), 1)
    before = jnp.where(same & (first < second), 1.0, 0.0)
    position = jnp.sum(before, axis=0, keepdims=True)
    target_ref[...] = (owner * cap + position).astype(jnp.int32)
    peer = lax.broadcasted_iota(jnp.int32, (peers, slots), 0).astype(jnp.float32)
    of_peer = jnp.where(peer == owner, 1.0, 0.0).astype(jnp.bfloat16)
    lane = lax.broadcasted_iota(jnp.int32, (slots, lanes), 1).astype(jnp.float32)
    here = to_column(position) == lane
    high = to_column((local >> 5).astype(jnp.float32))
    low = to_column((local & 31).astype(jnp.float32))
    parts = jnp.concatenate(
        [jnp.where(here, high, 0.0), jnp.where(here, low, 0.0)], axis=1
    ).astype(jnp.bfloat16)
    found = jnp.dot(of_peer, parts, preferred_element_type=jnp.float32)
    ask_ref[:, 0, :] = (found[:, :lanes] * 32.0 + found[:, lanes:]).astype(jnp.int32)


def request(owner, local, peers, cap):
    slots = owner.shape[1]
    return pl.pallas_call(
        functools.partial(request_kernel, cap=cap),
        out_shape=[
            jax.ShapeDtypeStruct((peers, 1, 128), jnp.int32),
            jax.ShapeDtypeStruct((1, slots), jnp.int32),
        ],
    )(owner, local)


def lookup_kernel(asked_ref, table_ref, out_ref, *, cap):
    peers = asked_ref.shape[0]
    lanes = asked_ref.shape[2]
    held = table_ref.shape[0]
    count = out_ref.shape[0]
    asked = asked_ref[:, 0, :]
    parts = jnp.concatenate(
        [(asked >> 5).astype(jnp.float32), (asked & 31).astype(jnp.float32)], axis=1
    ).astype(jnp.bfloat16)
    place = lax.broadcasted_iota(jnp.int32, (count, peers), 0)
    peer = lax.broadcasted_iota(jnp.int32, (count, peers), 1)
    spread = jnp.where(place // cap == peer, 1.0, 0.0).astype(jnp.bfloat16)
    both = jnp.dot(spread, parts, preferred_element_type=jnp.float32)
    both = both[:, :lanes] * 32.0 + both[:, lanes:]
    place = lax.broadcasted_iota(jnp.int32, (count, lanes), 0)
    lane = lax.broadcasted_iota(jnp.int32, (count, lanes), 1)
    wanted = jnp.sum(jnp.where(place % cap == lane, both, 0.0), axis=1, keepdims=True)
    column = lax.broadcasted_iota(jnp.int32, (count, held), 1).astype(jnp.float32)
    pick = jnp.where(wanted == column, 1.0, 0.0).astype(jnp.bfloat16)
    out_ref[...] = jnp.dot(
        pick, table_ref[...], preferred_element_type=jnp.float32
    ).astype(jnp.bfloat16)


def lookup(asked, table, cap):
    count = asked.shape[0] * cap
    return pl.pallas_call(
        functools.partial(lookup_kernel, cap=cap),
        out_shape=jax.ShapeDtypeStruct((count, table.shape[1]), jnp.bfloat16),
        compiler_params=pltpu.CompilerParams(vmem_limit_bytes=24 * 1024 * 1024),
        cost_estimate=pl.CostEstimate(
            flops=2 * count * table.size, bytes_accessed=4 * table.size, transcendentals=0
        ),
    )(asked, table)


def compact_kernel(back_ref, target_ref, rank_ref, out_ref):
    slots = target_ref.shape[1]
    held = back_ref.shape[0]
    width = back_ref.shape[1]
    column = to_column(target_ref[...].astype(jnp.float32))[:, :1]
    place = lax.broadcasted_iota(jnp.int32, (slots, held), 1).astype(jnp.float32)
    pick = (column == place).astype(jnp.bfloat16)
    out_ref[0:slots, :] = jnp.dot(
        pick, back_ref[...], preferred_element_type=jnp.float32
    ).astype(jnp.bfloat16)
    rank = rank_ref[...]
    high = (rank >> 7).astype(jnp.float32)
    low = (rank & 127).astype(jnp.float32)
    line = jnp.concatenate(
        [high, low, jnp.zeros((1, width - 2 * slots), jnp.float32)], axis=1
    )
    out_ref[slots : slots + EXTRA, :] = jnp.broadcast_to(line, (EXTRA, width)).astype(
        jnp.bfloat16
    )


def compact(back, target, rank):
    slots = target.shape[1]
    return pl.pallas_call(
        compact_kernel,
        out_shape=jax.ShapeDtypeStruct((slots + EXTRA, back.shape[1]), jnp.bfloat16),
        compiler_params=pltpu.CompilerParams(vmem_limit_bytes=24 * 1024 * 1024),
        cost_estimate=pl.CostEstimate(
            flops=2 * slots * back.shape[0] * back.shape[1],
            bytes_accessed=4 * back.size,
            transcendentals=0,
        ),
    )(back, target, rank)


def rank_row(ref, slots):
    line = ref[slots : slots + EXTRA, :][0:1].astype(jnp.float32)
    return line[:, 0:slots] * 128.0 + line[:, slots : 2 * slots]


def scores_of(row_refs, col_refs, col_only, with_col, slots):
    col_rank = [rank_row(ref, slots) for ref in col_refs]
    col_best = [jnp.full((8, slots), -1.0, jnp.float32) for _ in col_refs]
    row_best = []
    for row_ref in row_refs:
        own = to_column(rank_row(row_ref, slots))
        own = jnp.concatenate([own] * (slots // 128), axis=1)
        best = jnp.full((slots, 128), -1.0, jnp.float32)
        for i, col_ref in enumerate(col_refs):
            score = lax.dot_general(
                row_ref[0:slots, :],
                col_ref[0:slots, :],
                (((1,), (1,)), ((), ())),
                preferred_element_type=jnp.float32,
            )
            if not col_only:
                masked = jnp.where(col_rank[i] < own, score, -1.0)
                for k in range(slots // 128):
                    best = jnp.maximum(best, masked[:, 128 * k : 128 * (k + 1)])
            if with_col[i]:
                masked = jnp.where(own < col_rank[i], score, -1.0)
                folded = jnp.max(masked.reshape(slots // 8, 8, slots), axis=0)
                col_best[i] = jnp.maximum(col_best[i], folded)
        row_best.append(None if col_only else jnp.max(best.T, axis=0, keepdims=True))
    kept = [
        jnp.max(best, axis=0, keepdims=True)
        for best, wanted in zip(col_best, with_col)
        if wanted
    ]
    return row_best, kept


def first_kernel(*refs, slots):
    own_out, other_out, col_out = refs[10:]
    rows, cols = scores_of(refs[:6], refs[6:10], False, (False, True, True, True), slots)
    for j in range(3):
        own_out[j : j + 1, :] = rows[j]
        other_out[j : j + 1, :] = rows[j + 3]
        col_out[j : j + 1, :] = cols[j]


def last_kernel(*refs, slots):
    col_in, row_out, col_out = refs[13:]
    rows, cols = scores_of(refs[6:8], refs[8:12], False, (False, True, True, True), slots)
    _, far = scores_of(refs[:8], refs[12:13], True, (True,), slots)
    for j in range(2):
        row_out[j : j + 1, :] = rows[j]
    for j in range(3):
        col_out[j : j + 1, :] = jnp.maximum(col_in[j : j + 1, :], cols[j])
    col_out[3:4, :] = far[0]


def score(kernel, blocks, extra, shapes, pairs):
    slots = blocks[0].shape[0] - EXTRA
    width = blocks[0].shape[1]
    return pl.pallas_call(
        functools.partial(kernel, slots=slots),
        out_shape=[jax.ShapeDtypeStruct((n, slots), jnp.float32) for n in shapes],
        compiler_params=pltpu.CompilerParams(vmem_limit_bytes=40 * 1024 * 1024),
        cost_estimate=pl.CostEstimate(
            flops=2 * pairs * slots * slots * width,
            bytes_accessed=2 * len(blocks) * slots * width,
            transcendentals=0,
        ),
    )(*blocks, *extra)


def on_device(embeddings, storage_owner, local_row, member_rank, cluster_size):
    n_store = lax.axis_size("store")
    n_tile = lax.axis_size("tile")
    peers = n_store * n_tile
    slots = local_row.shape[1]
    width = embeddings.shape[1]
    cap = 2 * slots // peers
    both = ("store", "tile")
    s_index = lax.axis_index("store")
    t_index = lax.axis_index("tile")

    requests, target = request(storage_owner[:, :, 0], local_row, peers, cap)
    asked = lax.all_to_all(requests, both, split_axis=0, concat_axis=0, tiled=True)
    own_slot = (s_index * n_tile + t_index) * slots + jnp.arange(slots, dtype=jnp.int32)
    live = (own_slot < cluster_size[0])[None]
    rank = jnp.where(live, member_rank, jnp.int32(peers * slots))
    table = unit_rows(embeddings)
    found = lookup(asked, table, cap).reshape(peers, cap, width)
    back = lax.all_to_all(found, both, split_axis=0, concat_axis=0, tiled=True)
    block = compact(back.reshape(peers * cap, width), target, rank)

    def z_move(array, by):
        return lax.ppermute(
            array, "store", [(i, (i + by) % n_store) for i in range(n_store)]
        )

    def t_move(array, flip):
        return lax.ppermute(array, "tile", [(i, i ^ flip) for i in range(n_tile)])

    def zt_move(array, z_by, flip):
        pairs = []
        for z in range(n_store):
            for i in range(n_tile):
                pairs.append((z * n_tile + i, (z + z_by) % n_store * n_tile + (i ^ flip)))
        return lax.ppermute(array, both, pairs)

    near = z_move(block, -1)
    back_one = z_move(block, 1)
    near, back_one = lax.optimization_barrier((near, back_one))
    back_two = z_move(back_one, 1)
    x_one = t_move(near, 2)
    x_three = t_move(near, 6)
    near_other = t_move(near, 1)
    back_two, x_one, x_three = lax.optimization_barrier((back_two, x_one, x_three))
    back_three = z_move(back_two, 1)
    x_two = t_move(x_one, 6)
    x_one_other = t_move(x_one, 1)
    x_three_other = t_move(x_three, 1)
    x_two_other = t_move(x_three_other, 2)
    back_three, x_two, x_two_other = lax.optimization_barrier(
        (back_three, x_two, x_two_other)
    )

    cols = [near, block, back_one, back_two]
    early = [near, x_one, x_three, near_other, x_one_other, x_three_other]
    late = [x_two, x_two_other]
    mine, other, col_best = score(first_kernel, early + cols, [], [3, 3, 3], 24)
    mine = jnp.maximum(mine, t_move(other, 1))
    far, col_best = score(
        last_kernel, early + late + cols + [back_three], [col_best], [2, 4], 16
    )
    parts = [
        col_best[0:1],
        z_move(col_best[1:2], -1),
        z_move(col_best[2:3], -2),
        z_move(col_best[3:4], -3),
        zt_move(mine[0:1], 1, 0),
        zt_move(mine[1:2], 1, 2),
        zt_move(mine[2:3], 1, 6),
        zt_move(far[0:1], 1, 4),
        zt_move(far[1:2], 1, 5),
    ]
    highest = functools.reduce(jnp.maximum, parts)
    return jnp.where(live, highest, jnp.float32(0.0))


def solution(mesh):
    placed = (
        P(("store", "tile"), None),
        P("grp", ("store", "tile"), None),
        P("grp", ("store", "tile")),
        P("grp", ("store", "tile")),
        P("grp"),
    )
    return jax.shard_map(
        on_device,
        mesh=mesh,
        in_specs=placed,
        out_specs=P("grp", ("store", "tile")),
        check_vma=False,
    )
```

```python
import functools

import jax
import jax.numpy as jnp
from jax import lax
from jax.experimental import pallas as pl
from jax.experimental.pallas import tpu as pltpu
from jax.sharding import PartitionSpec as P

EXTRA = 16


def unit_rows(table):
    wide = table.astype(jnp.float32)
    total = jnp.sum(wide * wide, axis=-1, keepdims=True) + 1e-06
    return (wide * lax.rsqrt(total)).astype(jnp.bfloat16)


def to_column(row):
    return jnp.broadcast_to(row, (128, row.shape[1])).T


def request_kernel(owner_ref, local_ref, ask_ref, target_ref, *, cap):
    slots = owner_ref.shape[1]
    peers = ask_ref.shape[0]
    lanes = ask_ref.shape[2]
    owner = owner_ref[...].astype(jnp.float32)
    local = local_ref[...]
    column = to_column(owner)
    same = jnp.concatenate([column] * (slots // 128), axis=1) == owner
    first = lax.broadcasted_iota(jnp.int32, (slots, slots), 0)
    second = lax.broadcasted_iota(jnp.int32, (slots, slots), 1)
    before = jnp.where(same & (first < second), 1.0, 0.0)
    position = jnp.sum(before, axis=0, keepdims=True)
    target_ref[...] = (owner * cap + position).astype(jnp.int32)
    peer = lax.broadcasted_iota(jnp.int32, (peers, slots), 0).astype(jnp.float32)
    of_peer = jnp.where(peer == owner, 1.0, 0.0).astype(jnp.bfloat16)
    lane = lax.broadcasted_iota(jnp.int32, (slots, lanes), 1).astype(jnp.float32)
    here = to_column(position) == lane
    high = to_column((local >> 5).astype(jnp.float32))
    low = to_column((local & 31).astype(jnp.float32))
    parts = jnp.concatenate(
        [jnp.where(here, high, 0.0), jnp.where(here, low, 0.0)], axis=1
    ).astype(jnp.bfloat16)
    found = jnp.dot(of_peer, parts, preferred_element_type=jnp.float32)
    ask_ref[:, 0, :] = (found[:, :lanes] * 32.0 + found[:, lanes:]).astype(jnp.int32)


def request(owner, local, peers, cap):
    slots = owner.shape[1]
    return pl.pallas_call(
        functools.partial(request_kernel, cap=cap),
        out_shape=[
            jax.ShapeDtypeStruct((peers, 1, 128), jnp.int32),
            jax.ShapeDtypeStruct((1, slots), jnp.int32),
        ],
    )(owner, local)


def lookup_kernel(asked_ref, table_ref, out_ref, *, cap):
    peers = asked_ref.shape[0]
    lanes = asked_ref.shape[2]
    held = table_ref.shape[0]
    count = out_ref.shape[0]
    asked = asked_ref[:, 0, :]
    parts = jnp.concatenate(
        [(asked >> 5).astype(jnp.float32), (asked & 31).astype(jnp.float32)], axis=1
    ).astype(jnp.bfloat16)
    place = lax.broadcasted_iota(jnp.int32, (count, peers), 0)
    peer = lax.broadcasted_iota(jnp.int32, (count, peers), 1)
    spread = jnp.where(place // cap == peer, 1.0, 0.0).astype(jnp.bfloat16)
    both = jnp.dot(spread, parts, preferred_element_type=jnp.float32)
    both = both[:, :lanes] * 32.0 + both[:, lanes:]
    place = lax.broadcasted_iota(jnp.int32, (count, lanes), 0)
    lane = lax.broadcasted_iota(jnp.int32, (count, lanes), 1)
    wanted = jnp.sum(jnp.where(place % cap == lane, both, 0.0), axis=1, keepdims=True)
    column = lax.broadcasted_iota(jnp.int32, (count, held), 1).astype(jnp.float32)
    pick = jnp.where(wanted == column, 1.0, 0.0).astype(jnp.bfloat16)
    out_ref[...] = jnp.dot(
        pick, table_ref[...], preferred_element_type=jnp.float32
    ).astype(jnp.bfloat16)


def lookup(asked, table, cap):
    count = asked.shape[0] * cap
    return pl.pallas_call(
        functools.partial(lookup_kernel, cap=cap),
        out_shape=jax.ShapeDtypeStruct((count, table.shape[1]), jnp.bfloat16),
        compiler_params=pltpu.CompilerParams(vmem_limit_bytes=24 * 1024 * 1024),
        cost_estimate=pl.CostEstimate(
            flops=2 * count * table.size, bytes_accessed=4 * table.size, transcendentals=0
        ),
    )(asked, table)


def compact_kernel(back_ref, target_ref, rank_ref, out_ref):
    slots = target_ref.shape[1]
    held = back_ref.shape[0]
    width = back_ref.shape[1]
    column = to_column(target_ref[...].astype(jnp.float32))[:, :1]
    place = lax.broadcasted_iota(jnp.int32, (slots, held), 1).astype(jnp.float32)
    pick = (column == place).astype(jnp.bfloat16)
    out_ref[0:slots, :] = jnp.dot(
        pick, back_ref[...], preferred_element_type=jnp.float32
    ).astype(jnp.bfloat16)
    rank = rank_ref[...]
    high = (rank >> 7).astype(jnp.float32)
    low = (rank & 127).astype(jnp.float32)
    line = jnp.concatenate(
        [high, low, jnp.zeros((1, width - 2 * slots), jnp.float32)], axis=1
    )
    out_ref[slots : slots + EXTRA, :] = jnp.broadcast_to(line, (EXTRA, width)).astype(
        jnp.bfloat16
    )


def compact(back, target, rank):
    slots = target.shape[1]
    return pl.pallas_call(
        compact_kernel,
        out_shape=jax.ShapeDtypeStruct((slots + EXTRA, back.shape[1]), jnp.bfloat16),
        compiler_params=pltpu.CompilerParams(vmem_limit_bytes=24 * 1024 * 1024),
        cost_estimate=pl.CostEstimate(
            flops=2 * slots * back.shape[0] * back.shape[1],
            bytes_accessed=4 * back.size,
            transcendentals=0,
        ),
    )(back, target, rank)


def rank_row(ref, slots):
    line = ref[slots : slots + EXTRA, :][0:1].astype(jnp.float32)
    return line[:, 0:slots] * 128.0 + line[:, slots : 2 * slots]


def scores_of(row_refs, col_refs, col_only, with_col, slots):
    col_rank = [rank_row(ref, slots) for ref in col_refs]
    col_best = [jnp.full((8, slots), -1.0, jnp.float32) for _ in col_refs]
    row_best = []
    for row_ref in row_refs:
        own = to_column(rank_row(row_ref, slots))
        own = jnp.concatenate([own] * (slots // 128), axis=1)
        best = jnp.full((slots, 128), -1.0, jnp.float32)
        for i, col_ref in enumerate(col_refs):
            score = lax.dot_general(
                row_ref[0:slots, :],
                col_ref[0:slots, :],
                (((1,), (1,)), ((), ())),
                preferred_element_type=jnp.float32,
            )
            if not col_only:
                masked = jnp.where(col_rank[i] < own, score, -1.0)
                for k in range(slots // 128):
                    best = jnp.maximum(best, masked[:, 128 * k : 128 * (k + 1)])
            if with_col[i]:
                masked = jnp.where(own < col_rank[i], score, -1.0)
                folded = jnp.max(masked.reshape(slots // 8, 8, slots), axis=0)
                col_best[i] = jnp.maximum(col_best[i], folded)
        row_best.append(None if col_only else jnp.max(best.T, axis=0, keepdims=True))
    kept = [
        jnp.max(best, axis=0, keepdims=True)
        for best, wanted in zip(col_best, with_col)
        if wanted
    ]
    return row_best, kept


def first_kernel(*refs, slots):
    own_out, other_out, col_out = refs[10:]
    rows, cols = scores_of(refs[:6], refs[6:10], False, (False, True, True, True), slots)
    for j in range(3):
        own_out[j : j + 1, :] = rows[j]
        other_out[j : j + 1, :] = rows[j + 3]
        col_out[j : j + 1, :] = cols[j]


def second_kernel(*refs, slots):
    col_in, row_out, col_out = refs[6:]
    rows, cols = scores_of(refs[:2], refs[2:6], False, (False, True, True, True), slots)
    for j in range(2):
        row_out[j : j + 1, :] = rows[j]
    for j in range(3):
        col_out[j : j + 1, :] = jnp.maximum(col_in[j : j + 1, :], cols[j])


def last_kernel(*refs, slots):
    _, cols = scores_of(refs[:8], refs[8:9], True, (True,), slots)
    refs[9][...] = cols[0]


def score(kernel, blocks, extra, shapes, pairs):
    slots = blocks[0].shape[0] - EXTRA
    width = blocks[0].shape[1]
    return pl.pallas_call(
        functools.partial(kernel, slots=slots),
        out_shape=[jax.ShapeDtypeStruct((n, slots), jnp.float32) for n in shapes],
        compiler_params=pltpu.CompilerParams(vmem_limit_bytes=40 * 1024 * 1024),
        cost_estimate=pl.CostEstimate(
            flops=2 * pairs * slots * slots * width,
            bytes_accessed=2 * len(blocks) * slots * width,
            transcendentals=0,
        ),
    )(*blocks, *extra)


def on_device(embeddings, storage_owner, local_row, member_rank, cluster_size):
    n_store = lax.axis_size("store")
    n_tile = lax.axis_size("tile")
    peers = n_store * n_tile
    slots = local_row.shape[1]
    width = embeddings.shape[1]
    cap = 2 * slots // peers
    both = ("store", "tile")
    s_index = lax.axis_index("store")
    t_index = lax.axis_index("tile")

    requests, target = request(storage_owner[:, :, 0], local_row, peers, cap)
    asked = lax.all_to_all(requests, both, split_axis=0, concat_axis=0, tiled=True)
    own_slot = (s_index * n_tile + t_index) * slots + jnp.arange(slots, dtype=jnp.int32)
    live = (own_slot < cluster_size[0])[None]
    rank = jnp.where(live, member_rank, jnp.int32(peers * slots))
    table = unit_rows(embeddings)
    found = lookup(asked, table, cap).reshape(peers, cap, width)
    back = lax.all_to_all(found, both, split_axis=0, concat_axis=0, tiled=True)
    block = compact(back.reshape(peers * cap, width), target, rank)

    def z_move(array, by):
        return lax.ppermute(
            array, "store", [(i, (i + by) % n_store) for i in range(n_store)]
        )

    def t_move(array, flip):
        return lax.ppermute(array, "tile", [(i, i ^ flip) for i in range(n_tile)])

    def zt_move(array, z_by, flip):
        pairs = []
        for z in range(n_store):
            for i in range(n_tile):
                pairs.append((z * n_tile + i, (z + z_by) % n_store * n_tile + (i ^ flip)))
        return lax.ppermute(array, both, pairs)

    near = z_move(block, -1)
    back_one = z_move(block, 1)
    back_two = z_move(back_one, 1)
    x_one = t_move(near, 2)
    x_three = t_move(near, 6)
    near_other = t_move(near, 1)
    back_three = z_move(back_two, 1)
    x_two = t_move(x_one, 6)
    x_one_other = t_move(x_one, 1)
    x_three_other = t_move(x_three, 1)
    x_two_other = t_move(x_three_other, 2)
    cols = [near, block, back_one, back_two]
    early = [near, x_one, x_three, near_other, x_one_other, x_three_other]
    late = [x_two, x_two_other]
    mine, other, col_best = score(first_kernel, early + cols, [], [3, 3, 3], 24)
    mine = jnp.maximum(mine, t_move(other, 1))
    far, col_best = score(second_kernel, late + cols, [col_best], [2, 3], 8)
    (col_last,) = score(last_kernel, early + late + [back_three], [], [1], 8)
    passed = t_move(mine[1:3], 2)
    last = jnp.maximum(z_move(col_last, -1), col_best[2:3])
    parts = [
        col_best[0:1],
        z_move(col_best[1:2], -1),
        z_move(last, -2),
        zt_move(jnp.maximum(mine[0:1], passed[0:1]), 1, 0),
        zt_move(jnp.maximum(far[0:1], passed[1:2]), 1, 4),
        zt_move(far[1:2], 1, 5),
    ]
    highest = functools.reduce(jnp.maximum, parts)
    return jnp.where(live, highest, jnp.float32(0.0))


def solution(mesh):
    placed = (
        P(("store", "tile"), None),
        P("grp", ("store", "tile"), None),
        P("grp", ("store", "tile")),
        P("grp", ("store", "tile")),
        P("grp"),
    )
    return jax.shard_map(
        on_device,
        mesh=mesh,
        in_specs=placed,
        out_specs=P("grp", ("store", "tile")),
        check_vma=False,
    )
```

```python
import functools

import jax
import jax.numpy as jnp
from jax import lax
from jax.experimental import pallas as pl
from jax.experimental.pallas import tpu as pltpu
from jax.sharding import PartitionSpec as P

EXTRA = 16


def unit_rows(table):
    wide = table.astype(jnp.float32)
    total = jnp.sum(wide * wide, axis=-1, keepdims=True) + 1e-06
    return (wide * lax.rsqrt(total)).astype(jnp.bfloat16)


def to_column(row):
    return jnp.broadcast_to(row, (128, row.shape[1])).T


def request_kernel(owner_ref, local_ref, ask_ref, target_ref, *, cap):
    slots = owner_ref.shape[1]
    peers = ask_ref.shape[0]
    lanes = ask_ref.shape[2]
    owner = owner_ref[...].astype(jnp.float32)
    local = local_ref[...]
    column = to_column(owner)
    same = jnp.concatenate([column] * (slots // 128), axis=1) == owner
    first = lax.broadcasted_iota(jnp.int32, (slots, slots), 0)
    second = lax.broadcasted_iota(jnp.int32, (slots, slots), 1)
    before = jnp.where(same & (first < second), 1.0, 0.0)
    position = jnp.sum(before, axis=0, keepdims=True)
    target_ref[...] = (owner * cap + position).astype(jnp.int32)
    peer = lax.broadcasted_iota(jnp.int32, (peers, slots), 0).astype(jnp.float32)
    of_peer = jnp.where(peer == owner, 1.0, 0.0).astype(jnp.bfloat16)
    lane = lax.broadcasted_iota(jnp.int32, (slots, lanes), 1).astype(jnp.float32)
    here = to_column(position) == lane
    high = to_column((local >> 5).astype(jnp.float32))
    low = to_column((local & 31).astype(jnp.float32))
    parts = jnp.concatenate(
        [jnp.where(here, high, 0.0), jnp.where(here, low, 0.0)], axis=1
    ).astype(jnp.bfloat16)
    found = jnp.dot(of_peer, parts, preferred_element_type=jnp.float32)
    ask_ref[:, 0, :] = (found[:, :lanes] * 32.0 + found[:, lanes:]).astype(jnp.int32)


def request(owner, local, peers, cap):
    slots = owner.shape[1]
    return pl.pallas_call(
        functools.partial(request_kernel, cap=cap),
        out_shape=[
            jax.ShapeDtypeStruct((peers, 1, 128), jnp.int32),
            jax.ShapeDtypeStruct((1, slots), jnp.int32),
        ],
    )(owner, local)


def lookup_kernel(asked_ref, table_ref, out_ref, *, cap, chunk):
    lanes = asked_ref.shape[2]
    held = table_ref.shape[0]
    asked = asked_ref[:, 0, :lanes].astype(jnp.float32)
    lane = lax.broadcasted_iota(jnp.int32, (chunk, lanes), 1)
    place = lax.broadcasted_iota(jnp.int32, (chunk, lanes), 0)
    keep = lane == place % cap
    column = lax.broadcasted_iota(jnp.int32, (chunk, held), 1).astype(jnp.float32)
    group = chunk // cap
    for first in range(0, out_ref.shape[0], chunk):
        part = asked[first // cap : first // cap + group]
        part = jnp.broadcast_to(part[:, None, :], (group, cap, lanes))
        part = part.reshape(chunk, lanes)
        wanted = jnp.sum(jnp.where(keep, part, 0.0), axis=1, keepdims=True)
        pick = jnp.where(wanted == column, 1.0, 0.0).astype(jnp.bfloat16)
        out_ref[first : first + chunk, :] = jnp.dot(
            pick, table_ref[...], preferred_element_type=jnp.float32
        ).astype(jnp.bfloat16)


def lookup(asked, table, cap):
    count = asked.shape[0] * cap
    return pl.pallas_call(
        functools.partial(lookup_kernel, cap=cap, chunk=count // 2),
        out_shape=jax.ShapeDtypeStruct((count, table.shape[1]), jnp.bfloat16),
        compiler_params=pltpu.CompilerParams(vmem_limit_bytes=24 * 1024 * 1024),
        cost_estimate=pl.CostEstimate(
            flops=2 * count * table.size, bytes_accessed=4 * table.size, transcendentals=0
        ),
    )(asked, table)


def compact_kernel(back_ref, target_ref, rank_ref, out_ref):
    slots = target_ref.shape[1]
    held = back_ref.shape[0]
    width = back_ref.shape[1]
    column = to_column(target_ref[...].astype(jnp.float32))[:, :1]
    place = lax.broadcasted_iota(jnp.int32, (slots, held), 1).astype(jnp.float32)
    pick = (column == place).astype(jnp.bfloat16)
    out_ref[0:slots, :] = jnp.dot(
        pick, back_ref[...], preferred_element_type=jnp.float32
    ).astype(jnp.bfloat16)
    rank = rank_ref[...]
    high = (rank >> 7).astype(jnp.float32)
    low = (rank & 127).astype(jnp.float32)
    line = jnp.concatenate(
        [high, low, jnp.zeros((1, width - 2 * slots), jnp.float32)], axis=1
    )
    out_ref[slots : slots + EXTRA, :] = jnp.broadcast_to(line, (EXTRA, width)).astype(
        jnp.bfloat16
    )


def compact(back, target, rank):
    slots = target.shape[1]
    return pl.pallas_call(
        compact_kernel,
        out_shape=jax.ShapeDtypeStruct((slots + EXTRA, back.shape[1]), jnp.bfloat16),
        compiler_params=pltpu.CompilerParams(vmem_limit_bytes=24 * 1024 * 1024),
        cost_estimate=pl.CostEstimate(
            flops=2 * slots * back.shape[0] * back.shape[1],
            bytes_accessed=4 * back.size,
            transcendentals=0,
        ),
    )(back, target, rank)


def rank_row(ref, slots):
    line = ref[slots : slots + EXTRA, :][0:1].astype(jnp.float32)
    return line[:, 0:slots] * 128.0 + line[:, slots : 2 * slots]


def scores_of(row_refs, col_refs, col_only, with_col, slots):
    col_rank = [rank_row(ref, slots) for ref in col_refs]
    col_best = [jnp.full((8, slots), -1.0, jnp.float32) for _ in col_refs]
    row_best = []
    for row_ref in row_refs:
        own = to_column(rank_row(row_ref, slots))
        own = jnp.concatenate([own] * (slots // 128), axis=1)
        best = jnp.full((slots, 128), -1.0, jnp.float32)
        for i, col_ref in enumerate(col_refs):
            score = lax.dot_general(
                row_ref[0:slots, :],
                col_ref[0:slots, :],
                (((1,), (1,)), ((), ())),
                preferred_element_type=jnp.float32,
            )
            if not col_only:
                masked = jnp.where(col_rank[i] < own, score, -1.0)
                for k in range(slots // 128):
                    best = jnp.maximum(best, masked[:, 128 * k : 128 * (k + 1)])
            if with_col[i]:
                masked = jnp.where(own < col_rank[i], score, -1.0)
                folded = jnp.max(masked.reshape(slots // 8, 8, slots), axis=0)
                col_best[i] = jnp.maximum(col_best[i], folded)
        row_best.append(None if col_only else jnp.max(best.T, axis=0, keepdims=True))
    kept = [
        jnp.max(best, axis=0, keepdims=True)
        for best, wanted in zip(col_best, with_col)
        if wanted
    ]
    return row_best, kept


def first_kernel(*refs, slots):
    own_out, other_out, col_out = refs[10:]
    rows, cols = scores_of(refs[:6], refs[6:10], False, (False, True, True, True), slots)
    for j in range(3):
        own_out[j : j + 1, :] = rows[j]
        other_out[j : j + 1, :] = rows[j + 3]
        col_out[j : j + 1, :] = cols[j]


def second_kernel(*refs, slots):
    col_in, row_out, col_out = refs[6:]
    rows, cols = scores_of(refs[:2], refs[2:6], False, (False, True, True, True), slots)
    for j in range(2):
        row_out[j : j + 1, :] = rows[j]
    for j in range(3):
        col_out[j : j + 1, :] = jnp.maximum(col_in[j : j + 1, :], cols[j])


def last_kernel(*refs, slots):
    _, cols = scores_of(refs[:8], refs[8:9], True, (True,), slots)
    refs[9][...] = cols[0]


def score(kernel, blocks, extra, shapes, pairs):
    slots = blocks[0].shape[0] - EXTRA
    width = blocks[0].shape[1]
    return pl.pallas_call(
        functools.partial(kernel, slots=slots),
        out_shape=[jax.ShapeDtypeStruct((n, slots), jnp.float32) for n in shapes],
        compiler_params=pltpu.CompilerParams(vmem_limit_bytes=40 * 1024 * 1024),
        cost_estimate=pl.CostEstimate(
            flops=2 * pairs * slots * slots * width,
            bytes_accessed=2 * len(blocks) * slots * width,
            transcendentals=0,
        ),
    )(*blocks, *extra)


def on_device(embeddings, storage_owner, local_row, member_rank, cluster_size):
    n_store = lax.axis_size("store")
    n_tile = lax.axis_size("tile")
    peers = n_store * n_tile
    slots = local_row.shape[1]
    width = embeddings.shape[1]
    cap = 2 * slots // peers
    both = ("store", "tile")
    s_index = lax.axis_index("store")
    t_index = lax.axis_index("tile")

    requests, target = request(storage_owner[:, :, 0], local_row, peers, cap)
    asked = lax.all_to_all(requests, both, split_axis=0, concat_axis=0, tiled=True)
    own_slot = (s_index * n_tile + t_index) * slots + jnp.arange(slots, dtype=jnp.int32)
    live = (own_slot < cluster_size[0])[None]
    rank = jnp.where(live, member_rank, jnp.int32(peers * slots))
    table = unit_rows(embeddings)
    found = lookup(asked, table, cap).reshape(peers, cap, width)
    back = lax.all_to_all(found, both, split_axis=0, concat_axis=0, tiled=True)
    block = compact(back.reshape(peers * cap, width), target, rank)

    def z_move(array, by):
        return lax.ppermute(
            array, "store", [(i, (i + by) % n_store) for i in range(n_store)]
        )

    def t_move(array, flip):
        return lax.ppermute(array, "tile", [(i, i ^ flip) for i in range(n_tile)])

    def zt_move(array, z_by, flip):
        pairs = []
        for z in range(n_store):
            for i in range(n_tile):
                pairs.append((z * n_tile + i, (z + z_by) % n_store * n_tile + (i ^ flip)))
        return lax.ppermute(array, both, pairs)

    near = z_move(block, -1)
    back_one = z_move(block, 1)
    back_two = z_move(back_one, 1)
    x_one = t_move(near, 2)
    x_three = t_move(near, 6)
    near_other = t_move(near, 1)
    back_three = z_move(back_two, 1)
    x_two = t_move(x_one, 6)
    x_one_other = t_move(x_one, 1)
    x_three_other = t_move(x_three, 1)
    x_two_other = t_move(x_three_other, 2)
    cols = [near, block, back_one, back_two]
    early = [near, x_one, x_three, near_other, x_one_other, x_three_other]
    late = [x_two, x_two_other]
    mine, other, col_best = score(first_kernel, early + cols, [], [3, 3, 3], 24)
    mine = jnp.maximum(mine, t_move(other, 1))
    far, col_best = score(second_kernel, late + cols, [col_best], [2, 3], 8)
    (col_last,) = score(last_kernel, early + late + [back_three], [], [1], 8)
    passed = t_move(mine[1:3], 2)
    last = jnp.maximum(z_move(col_last, -1), col_best[2:3])
    parts = [
        col_best[0:1],
        z_move(col_best[1:2], -1),
        z_move(last, -2),
        zt_move(jnp.maximum(mine[0:1], passed[0:1]), 1, 0),
        zt_move(jnp.maximum(far[0:1], passed[1:2]), 1, 4),
        zt_move(far[1:2], 1, 5),
    ]
    highest = functools.reduce(jnp.maximum, parts)
    return jnp.where(live, highest, jnp.float32(0.0))


def solution(mesh):
    placed = (
        P(("store", "tile"), None),
        P("grp", ("store", "tile"), None),
        P("grp", ("store", "tile")),
        P("grp", ("store", "tile")),
        P("grp"),
    )
    return jax.shard_map(
        on_device,
        mesh=mesh,
        in_specs=placed,
        out_specs=P("grp", ("store", "tile")),
        check_vma=False,
    )
```

```python
import functools

import jax
import jax.numpy as jnp
from jax import lax
from jax.experimental import pallas as pl
from jax.experimental.pallas import tpu as pltpu
from jax.sharding import PartitionSpec as P

DEAD = 1 << 15


def unit_rows(table):
    wide = table.astype(jnp.float32)
    total = jnp.sum(wide * wide, axis=-1, keepdims=True) + 1e-06
    return (wide * lax.rsqrt(total)).astype(jnp.bfloat16)


def to_column(row):
    return jnp.broadcast_to(row, (128, row.shape[1])).T


def request_kernel(count_ref, owner_ref, local_ref, rank_ref, ask_ref, target_ref, *, cap):
    slots = owner_ref.shape[1]
    peers = ask_ref.shape[0]
    lanes = ask_ref.shape[2] // 2
    owner = owner_ref[...].astype(jnp.float32)
    local = local_ref[...]
    column = to_column(owner)
    same = jnp.concatenate([column] * (slots // 128), axis=1) == owner
    first = lax.broadcasted_iota(jnp.int32, (slots, slots), 0)
    second = lax.broadcasted_iota(jnp.int32, (slots, slots), 1)
    before = jnp.where(same & (first < second), 1.0, 0.0)
    position = jnp.sum(before, axis=0, keepdims=True)
    target_ref[...] = (owner * cap + position).astype(jnp.int32)
    peer = lax.broadcasted_iota(jnp.int32, (peers, slots), 0).astype(jnp.float32)
    of_peer = jnp.where(peer == owner, 1.0, 0.0).astype(jnp.bfloat16)
    lane = lax.broadcasted_iota(jnp.int32, (slots, lanes), 1).astype(jnp.float32)
    here = to_column(position) == lane
    high = to_column((local >> 5).astype(jnp.float32))
    low = to_column((local & 31).astype(jnp.float32))
    parts = jnp.concatenate(
        [jnp.where(here, high, 0.0), jnp.where(here, low, 0.0)], axis=1
    ).astype(jnp.bfloat16)
    found = jnp.dot(of_peer, parts, preferred_element_type=jnp.float32)
    ask_ref[:, 0, :lanes] = (found[:, :lanes] * 32.0 + found[:, lanes:]).astype(jnp.int32)
    slot = lax.broadcasted_iota(jnp.int32, (1, slots), 1)
    rank = jnp.where(slot < count_ref[0], rank_ref[...], DEAD - 1)
    line = rank[:, :lanes] + rank[:, lanes:] * DEAD
    ask_ref[:, 0, lanes:] = jnp.broadcast_to(line, (peers, lanes))


def request(count, owner, local, rank, peers, cap):
    slots = owner.shape[1]
    return pl.pallas_call(
        functools.partial(request_kernel, cap=cap),
        out_shape=[
            jax.ShapeDtypeStruct((peers, 1, slots), jnp.int32),
            jax.ShapeDtypeStruct((1, slots), jnp.int32),
        ],
        in_specs=[pl.BlockSpec(memory_space=pltpu.SMEM)]
        + [pl.BlockSpec(memory_space=pltpu.VMEM)] * 3,
    )(count, owner, local, rank)


def lookup_kernel(asked_ref, table_ref, out_ref, *, cap, chunk):
    lanes = asked_ref.shape[2] // 2
    held = table_ref.shape[0]
    asked = asked_ref[:, 0, :lanes].astype(jnp.float32)
    lane = lax.broadcasted_iota(jnp.int32, (chunk, lanes), 1)
    place = lax.broadcasted_iota(jnp.int32, (chunk, lanes), 0)
    keep = lane == place % cap
    column = lax.broadcasted_iota(jnp.int32, (chunk, held), 1).astype(jnp.float32)
    group = chunk // cap
    for first in range(0, out_ref.shape[0], chunk):
        part = asked[first // cap : first // cap + group]
        part = jnp.broadcast_to(part[:, None, :], (group, cap, lanes))
        part = part.reshape(chunk, lanes)
        wanted = jnp.sum(jnp.where(keep, part, 0.0), axis=1, keepdims=True)
        pick = jnp.where(wanted == column, 1.0, 0.0).astype(jnp.bfloat16)
        out_ref[first : first + chunk, :] = jnp.dot(
            pick, table_ref[...], preferred_element_type=jnp.float32
        ).astype(jnp.bfloat16)


def lookup(asked, table, cap):
    count = asked.shape[0] * cap
    return pl.pallas_call(
        functools.partial(lookup_kernel, cap=cap, chunk=count // 2),
        out_shape=jax.ShapeDtypeStruct((count, table.shape[1]), jnp.bfloat16),
        compiler_params=pltpu.CompilerParams(vmem_limit_bytes=24 * 1024 * 1024),
        cost_estimate=pl.CostEstimate(
            flops=2 * count * table.size, bytes_accessed=4 * table.size, transcendentals=0
        ),
    )(asked, table)


def compact_kernel(back_ref, target_ref, out_ref):
    slots = target_ref.shape[1]
    held = back_ref.shape[0]
    column = to_column(target_ref[...].astype(jnp.float32))[:, :1]
    place = lax.broadcasted_iota(jnp.int32, (slots, held), 1).astype(jnp.float32)
    pick = (column == place).astype(jnp.bfloat16)
    out_ref[...] = jnp.dot(
        pick, back_ref[...], preferred_element_type=jnp.float32
    ).astype(jnp.bfloat16)


def compact(back, target):
    slots = target.shape[1]
    return pl.pallas_call(
        compact_kernel,
        out_shape=jax.ShapeDtypeStruct((slots, back.shape[1]), jnp.bfloat16),
        compiler_params=pltpu.CompilerParams(vmem_limit_bytes=24 * 1024 * 1024),
        cost_estimate=pl.CostEstimate(
            flops=2 * slots * back.shape[0] * back.shape[1],
            bytes_accessed=4 * back.size,
            transcendentals=0,
        ),
    )(back, target)


def scores_of(row_refs, row_at, col_refs, col_at, rank_ref, col_only, with_col):
    slots = rank_ref.shape[2]
    col_rank = [rank_ref[at] for at in col_at]
    col_best = [jnp.full((8, slots), -1.0, jnp.float32) for _ in col_refs]
    row_best = []
    for row_ref, at in zip(row_refs, row_at):
        own = to_column(rank_ref[at])
        own = jnp.concatenate([own] * (slots // 128), axis=1)
        best = jnp.full((slots, 128), -1.0, jnp.float32)
        for i, col_ref in enumerate(col_refs):
            score = lax.dot_general(
                row_ref[...],
                col_ref[...],
                (((1,), (1,)), ((), ())),
                preferred_element_type=jnp.float32,
            )
            if not col_only:
                masked = jnp.where(col_rank[i] < own, score, -1.0)
                for k in range(slots // 128):
                    best = jnp.maximum(best, masked[:, 128 * k : 128 * (k + 1)])
            if with_col[i]:
                masked = jnp.where(own < col_rank[i], score, -1.0)
                folded = jnp.max(masked.reshape(slots // 8, 8, slots), axis=0)
                col_best[i] = jnp.maximum(col_best[i], folded)
        row_best.append(None if col_only else jnp.max(best.T, axis=0, keepdims=True))
    kept = [
        jnp.max(best, axis=0, keepdims=True)
        for best, wanted in zip(col_best, with_col)
        if wanted
    ]
    return row_best, kept


COLS = (0, 8, 9, 10)
WITH_COL = (False, True, True, True)


def first_kernel(*refs):
    rank_ref, own_out, other_out, col_out = refs[10:]
    rows, cols = scores_of(
        refs[:6], range(6), refs[6:10], COLS, rank_ref, False, WITH_COL
    )
    for j in range(3):
        own_out[j : j + 1, :] = rows[j]
        other_out[j : j + 1, :] = rows[j + 3]
        col_out[j : j + 1, :] = cols[j]


def second_kernel(*refs):
    rank_ref, col_in, row_out, col_out = refs[6:]
    rows, cols = scores_of(refs[:2], (6, 7), refs[2:6], COLS, rank_ref, False, WITH_COL)
    for j in range(2):
        row_out[j : j + 1, :] = rows[j]
    for j in range(3):
        col_out[j : j + 1, :] = jnp.maximum(col_in[j : j + 1, :], cols[j])


def last_kernel(*refs):
    rank_ref, col_out = refs[9:]
    _, cols = scores_of(refs[:8], range(8), refs[8:9], (11,), rank_ref, True, (True,))
    col_out[...] = cols[0]


def score(kernel, blocks, extra, shapes, pairs):
    slots, width = blocks[0].shape
    return pl.pallas_call(
        kernel,
        out_shape=[jax.ShapeDtypeStruct((n, slots), jnp.float32) for n in shapes],
        compiler_params=pltpu.CompilerParams(vmem_limit_bytes=40 * 1024 * 1024),
        cost_estimate=pl.CostEstimate(
            flops=2 * pairs * slots * slots * width,
            bytes_accessed=2 * len(blocks) * slots * width,
            transcendentals=0,
        ),
    )(*blocks, *extra)


def on_device(embeddings, storage_owner, local_row, member_rank, cluster_size):
    n_store = lax.axis_size("store")
    n_tile = lax.axis_size("tile")
    peers = n_store * n_tile
    slots = local_row.shape[1]
    width = embeddings.shape[1]
    cap = 2 * slots // peers
    both = ("store", "tile")
    s_index = lax.axis_index("store")
    t_index = lax.axis_index("tile")

    first_slot = (s_index * n_tile + t_index) * slots
    count = cluster_size - first_slot
    requests, target = request(
        count, storage_owner[:, :, 0], local_row, member_rank, peers, cap
    )
    asked = lax.all_to_all(requests, both, split_axis=0, concat_axis=0, tiled=True)
    live = (jnp.arange(slots, dtype=jnp.int32) < count[0])[None]
    flips = jnp.array([0, 2, 6, 1, 3, 7, 4, 5], jnp.int32)
    near_at = (s_index + 1) % n_store * n_tile + (t_index ^ flips)
    col_at = (s_index - jnp.arange(4, dtype=jnp.int32)) % n_store * n_tile + t_index
    lines = jnp.take(
        asked[:, 0, slots // 2 :], jnp.concatenate([near_at, col_at]), axis=0
    )
    rank = jnp.concatenate([lines & (DEAD - 1), lines >> 15], axis=1)
    rank = rank.astype(jnp.float32)[:, None, :]
    table = unit_rows(embeddings)
    found = lookup(asked, table, cap).reshape(peers, cap, width)
    back = lax.all_to_all(found, both, split_axis=0, concat_axis=0, tiled=True)
    block = compact(back.reshape(peers * cap, width), target)

    def z_move(array, by):
        return lax.ppermute(
            array, "store", [(i, (i + by) % n_store) for i in range(n_store)]
        )

    def t_move(array, flip):
        return lax.ppermute(array, "tile", [(i, i ^ flip) for i in range(n_tile)])

    def zt_move(array, z_by, flip):
        pairs = []
        for z in range(n_store):
            for i in range(n_tile):
                pairs.append((z * n_tile + i, (z + z_by) % n_store * n_tile + (i ^ flip)))
        return lax.ppermute(array, both, pairs)

    near = z_move(block, -1)
    back_one = z_move(block, 1)
    back_two = z_move(back_one, 1)
    x_one = t_move(near, 2)
    x_three = t_move(near, 6)
    near_other = t_move(near, 1)
    back_three = z_move(back_two, 1)
    x_two = t_move(x_one, 6)
    x_one_other = t_move(x_one, 1)
    x_three_other = t_move(x_three, 1)
    x_two_other = t_move(x_three_other, 2)
    cols = [near, block, back_one, back_two]
    early = [near, x_one, x_three, near_other, x_one_other, x_three_other]
    late = [x_two, x_two_other]
    mine, other, col_best = score(first_kernel, early + cols, [rank], [3, 3, 3], 24)
    mine = jnp.maximum(mine, t_move(other, 1))
    far, col_best = score(second_kernel, late + cols, [rank, col_best], [2, 3], 8)
    (col_last,) = score(last_kernel, early + late + [back_three], [rank], [1], 8)
    passed = t_move(mine[1:3], 2)
    last = jnp.maximum(z_move(col_last, -1), col_best[2:3])
    parts = [
        col_best[0:1],
        z_move(col_best[1:2], -1),
        z_move(last, -2),
        zt_move(jnp.maximum(mine[0:1], passed[0:1]), 1, 0),
        zt_move(jnp.maximum(far[0:1], passed[1:2]), 1, 4),
        zt_move(far[1:2], 1, 5),
    ]
    highest = functools.reduce(jnp.maximum, parts)
    return jnp.where(live, highest, jnp.float32(0.0))


def solution(mesh):
    placed = (
        P(("store", "tile"), None),
        P("grp", ("store", "tile"), None),
        P("grp", ("store", "tile")),
        P("grp", ("store", "tile")),
        P("grp"),
    )
    return jax.shard_map(
        on_device,
        mesh=mesh,
        in_specs=placed,
        out_specs=P("grp", ("store", "tile")),
        check_vma=False,
    )
```

```python
import functools

import jax
import jax.numpy as jnp
from jax import lax
from jax.experimental import pallas as pl
from jax.experimental.pallas import tpu as pltpu
from jax.sharding import PartitionSpec as P

DEAD = 1 << 15


def unit_rows(table):
    wide = table.astype(jnp.float32)
    total = jnp.sum(wide * wide, axis=-1, keepdims=True) + 1e-06
    return (wide * lax.rsqrt(total)).astype(jnp.bfloat16)


def to_column(row):
    return jnp.broadcast_to(row, (128, row.shape[1])).T


def request_kernel(count_ref, owner_ref, local_ref, rank_ref, ask_ref, target_ref, *, cap):
    slots = owner_ref.shape[1]
    peers = ask_ref.shape[0]
    lanes = ask_ref.shape[2] // 2
    owner = owner_ref[...].astype(jnp.float32)
    local = local_ref[...]
    column = to_column(owner)
    same = jnp.concatenate([column] * (slots // 128), axis=1) == owner
    first = lax.broadcasted_iota(jnp.int32, (slots, slots), 0)
    second = lax.broadcasted_iota(jnp.int32, (slots, slots), 1)
    before = jnp.where(same & (first < second), 1.0, 0.0)
    position = jnp.sum(before, axis=0, keepdims=True)
    target_ref[...] = (owner * cap + position).astype(jnp.int32)
    peer = lax.broadcasted_iota(jnp.int32, (peers, slots), 0).astype(jnp.float32)
    of_peer = jnp.where(peer == owner, 1.0, 0.0).astype(jnp.bfloat16)
    lane = lax.broadcasted_iota(jnp.int32, (slots, lanes), 1).astype(jnp.float32)
    here = to_column(position) == lane
    high = to_column((local >> 5).astype(jnp.float32))
    low = to_column((local & 31).astype(jnp.float32))
    parts = jnp.concatenate(
        [jnp.where(here, high, 0.0), jnp.where(here, low, 0.0)], axis=1
    ).astype(jnp.bfloat16)
    found = jnp.dot(of_peer, parts, preferred_element_type=jnp.float32)
    ask_ref[:, 0, :lanes] = (found[:, :lanes] * 32.0 + found[:, lanes:]).astype(jnp.int32)
    slot = lax.broadcasted_iota(jnp.int32, (1, slots), 1)
    rank = jnp.where(slot < count_ref[0], rank_ref[...], DEAD - 1)
    line = rank[:, :lanes] + rank[:, lanes:] * DEAD
    ask_ref[:, 0, lanes:] = jnp.broadcast_to(line, (peers, lanes))


def request(count, owner, local, rank, peers, cap):
    slots = owner.shape[1]
    return pl.pallas_call(
        functools.partial(request_kernel, cap=cap),
        out_shape=[
            jax.ShapeDtypeStruct((peers, 1, slots), jnp.int32),
            jax.ShapeDtypeStruct((1, slots), jnp.int32),
        ],
        in_specs=[pl.BlockSpec(memory_space=pltpu.SMEM)]
        + [pl.BlockSpec(memory_space=pltpu.VMEM)] * 3,
    )(count, owner, local, rank)


def lookup_kernel(asked_ref, table_ref, out_ref, *, cap, chunk):
    lanes = asked_ref.shape[2] // 2
    held = table_ref.shape[0]
    asked = asked_ref[:, 0, :lanes].astype(jnp.float32)
    lane = lax.broadcasted_iota(jnp.int32, (chunk, lanes), 1)
    place = lax.broadcasted_iota(jnp.int32, (chunk, lanes), 0)
    keep = lane == place % cap
    column = lax.broadcasted_iota(jnp.int32, (chunk, held), 1).astype(jnp.float32)
    group = chunk // cap
    for first in range(0, out_ref.shape[0], chunk):
        part = asked[first // cap : first // cap + group]
        part = jnp.broadcast_to(part[:, None, :], (group, cap, lanes))
        part = part.reshape(chunk, lanes)
        wanted = jnp.sum(jnp.where(keep, part, 0.0), axis=1, keepdims=True)
        pick = jnp.where(wanted == column, 1.0, 0.0).astype(jnp.bfloat16)
        out_ref[first : first + chunk, :] = jnp.dot(
            pick, table_ref[...], preferred_element_type=jnp.float32
        ).astype(jnp.bfloat16)


def lookup(asked, table, cap):
    count = asked.shape[0] * cap
    return pl.pallas_call(
        functools.partial(lookup_kernel, cap=cap, chunk=count // 2),
        out_shape=jax.ShapeDtypeStruct((count, table.shape[1]), jnp.bfloat16),
        compiler_params=pltpu.CompilerParams(vmem_limit_bytes=24 * 1024 * 1024),
        cost_estimate=pl.CostEstimate(
            flops=2 * count * table.size, bytes_accessed=4 * table.size, transcendentals=0
        ),
    )(asked, table)


def compact_kernel(back_ref, target_ref, out_ref):
    slots = target_ref.shape[1]
    held = back_ref.shape[0]
    column = to_column(target_ref[...].astype(jnp.float32))[:, :1]
    place = lax.broadcasted_iota(jnp.int32, (slots, held), 1).astype(jnp.float32)
    pick = (column == place).astype(jnp.bfloat16)
    out_ref[...] = jnp.dot(
        pick, back_ref[...], preferred_element_type=jnp.float32
    ).astype(jnp.bfloat16)


def compact(back, target):
    slots = target.shape[1]
    return pl.pallas_call(
        compact_kernel,
        out_shape=jax.ShapeDtypeStruct((slots, back.shape[1]), jnp.bfloat16),
        compiler_params=pltpu.CompilerParams(vmem_limit_bytes=24 * 1024 * 1024),
        cost_estimate=pl.CostEstimate(
            flops=2 * slots * back.shape[0] * back.shape[1],
            bytes_accessed=4 * back.size,
            transcendentals=0,
        ),
    )(back, target)


def scores_of(row_refs, row_at, col_refs, col_at, rank_ref, col_only, with_col):
    slots = rank_ref.shape[2]
    col_rank = [rank_ref[at] for at in col_at]
    col_best = [jnp.full((8, slots), -1.0, jnp.float32) for _ in col_refs]
    row_best = []
    for row_ref, at in zip(row_refs, row_at):
        own = to_column(rank_ref[at])
        own = jnp.concatenate([own] * (slots // 128), axis=1)
        best = jnp.full((slots, 128), -1.0, jnp.float32)
        for i, col_ref in enumerate(col_refs):
            score = lax.dot_general(
                row_ref[...],
                col_ref[...],
                (((1,), (1,)), ((), ())),
                preferred_element_type=jnp.float32,
            )
            if not col_only:
                masked = jnp.where(col_rank[i] < own, score, -1.0)
                for k in range(slots // 128):
                    best = jnp.maximum(best, masked[:, 128 * k : 128 * (k + 1)])
            if with_col[i]:
                masked = jnp.where(own < col_rank[i], score, -1.0)
                folded = jnp.max(masked.reshape(slots // 8, 8, slots), axis=0)
                col_best[i] = jnp.maximum(col_best[i], folded)
        row_best.append(None if col_only else jnp.max(best.T, axis=0, keepdims=True))
    kept = [
        jnp.max(best, axis=0, keepdims=True)
        for best, wanted in zip(col_best, with_col)
        if wanted
    ]
    return row_best, kept


COLS = (0, 8, 9, 10)
WITH_COL = (False, True, True, True)


def first_kernel(*refs):
    rank_ref, own_out, other_out, col_out = refs[10:]
    rows, cols = scores_of(
        refs[:6], range(6), refs[6:10], COLS, rank_ref, False, WITH_COL
    )
    for j in range(3):
        own_out[j : j + 1, :] = rows[j]
        other_out[j : j + 1, :] = rows[j + 3]
        col_out[j : j + 1, :] = cols[j]


def second_kernel(*refs):
    rank_ref, col_in, row_out, col_out = refs[6:]
    rows, cols = scores_of(refs[:2], (6, 7), refs[2:6], COLS, rank_ref, False, WITH_COL)
    for j in range(2):
        row_out[j : j + 1, :] = rows[j]
    for j in range(3):
        col_out[j : j + 1, :] = jnp.maximum(col_in[j : j + 1, :], cols[j])


def last_kernel(*refs):
    rank_ref, col_out = refs[9:]
    _, cols = scores_of(refs[:8], range(8), refs[8:9], (11,), rank_ref, True, (True,))
    col_out[...] = cols[0]


def score(kernel, blocks, extra, shapes, pairs):
    slots, width = blocks[0].shape
    return pl.pallas_call(
        kernel,
        out_shape=[jax.ShapeDtypeStruct((n, slots), jnp.float32) for n in shapes],
        compiler_params=pltpu.CompilerParams(vmem_limit_bytes=40 * 1024 * 1024),
        cost_estimate=pl.CostEstimate(
            flops=2 * pairs * slots * slots * width,
            bytes_accessed=2 * len(blocks) * slots * width,
            transcendentals=0,
        ),
    )(*blocks, *extra)


def on_device(embeddings, storage_owner, local_row, member_rank, cluster_size):
    n_store = lax.axis_size("store")
    n_tile = lax.axis_size("tile")
    peers = n_store * n_tile
    slots = local_row.shape[1]
    width = embeddings.shape[1]
    cap = 2 * slots // peers
    both = ("store", "tile")
    s_index = lax.axis_index("store")
    t_index = lax.axis_index("tile")

    first_slot = (s_index * n_tile + t_index) * slots
    count = cluster_size - first_slot
    requests, target = request(
        count, storage_owner[:, :, 0], local_row, member_rank, peers, cap
    )
    asked = lax.all_to_all(requests, both, split_axis=0, concat_axis=0, tiled=True)
    live = (jnp.arange(slots, dtype=jnp.int32) < count[0])[None]
    flips = jnp.array([0, 2, 6, 1, 3, 7, 4, 5], jnp.int32)
    near_at = (s_index + 1) % n_store * n_tile + (t_index ^ flips)
    col_at = (s_index - jnp.arange(4, dtype=jnp.int32)) % n_store * n_tile + t_index
    lines = jnp.take(
        asked[:, 0, slots // 2 :], jnp.concatenate([near_at, col_at]), axis=0
    )
    rank = jnp.concatenate([lines & (DEAD - 1), lines >> 15], axis=1)
    rank = rank.astype(jnp.float32)[:, None, :]
    table = unit_rows(embeddings)
    found = lookup(asked, table, cap).reshape(peers, cap, width)
    back = lax.all_to_all(found, both, split_axis=0, concat_axis=0, tiled=True)
    block = compact(back.reshape(peers * cap, width), target)

    def z_move(array, by):
        return lax.ppermute(
            array, "store", [(i, (i + by) % n_store) for i in range(n_store)]
        )

    def t_move(array, flip):
        return lax.ppermute(array, "tile", [(i, i ^ flip) for i in range(n_tile)])

    near = z_move(block, -1)
    back_one = z_move(block, 1)
    back_two = z_move(back_one, 1)
    x_one = t_move(near, 2)
    x_three = t_move(near, 6)
    near_other = t_move(near, 1)
    back_three = z_move(back_two, 1)
    x_two = t_move(x_one, 6)
    x_one_other = t_move(x_one, 1)
    x_three_other = t_move(x_three, 1)
    x_two_other = t_move(x_three_other, 2)
    cols = [near, block, back_one, back_two]
    early = [near, x_one, x_three, near_other, x_one_other, x_three_other]
    late = [x_two, x_two_other]
    mine, other, col_best = score(first_kernel, early + cols, [rank], [3, 3, 3], 24)
    mine = jnp.maximum(mine, t_move(other, 1))
    (col_last,) = score(last_kernel, early + late + [back_three], [rank], [1], 8)
    _, col_best = lax.optimization_barrier((col_last, col_best))
    far, col_best = score(second_kernel, late + cols, [rank, col_best], [2, 3], 8)
    passed = t_move(mine[1:3], 2)
    across = jnp.maximum(far[0:1], passed[1:2])
    across = t_move(jnp.maximum(across, t_move(far[1:2], 1)), 4)
    first = jnp.maximum(jnp.maximum(mine[0:1], passed[0:1]), across)
    last = jnp.maximum(z_move(col_last, -1), col_best[2:3])
    parts = [
        col_best[0:1],
        z_move(col_best[1:2], -1),
        z_move(last, -2),
        z_move(first, 1),
    ]
    highest = functools.reduce(jnp.maximum, parts)
    return jnp.where(live, highest, jnp.float32(0.0))


def solution(mesh):
    placed = (
        P(("store", "tile"), None),
        P("grp", ("store", "tile"), None),
        P("grp", ("store", "tile")),
        P("grp", ("store", "tile")),
        P("grp"),
    )
    return jax.shard_map(
        on_device,
        mesh=mesh,
        in_specs=placed,
        out_specs=P("grp", ("store", "tile")),
        check_vma=False,
    )
```
